32 devices in a mesh: seq: 4 (over y, x), chan: 8 (over z, core).
Axes of the slice: x: 2, y: 2, z: 4, core: 2. Of those that a mesh axis runs over, the one named last changes fastest.
Arguments:
- conv_input: bfloat16 [4096, 4096], P('seq', 'chan'), may hold values from -0.0078125 to 0.0078125
- grad_out: bfloat16 [4096, 4096], P(('seq', 'chan')), may hold values from -6 to 6
- out_weight: bfloat16 [4096, 4096], P('chan'), may hold values from -0.09375 to 0.09375
- filters: bfloat16 [128, 8192], P('chan'), may hold values from -0.0625 to 0.0625
Outputs:
- grad_input: bfloat16 [4096, 4096], P('seq', 'chan')
- grad_filters: float32 [128, 8192], P('chan', 'seq')
The draws below stay inside these ranges and needn't reach their ends.
All inputs are finite; a program needn't handle non-finite values.
Results may differ from the reference program's by a relative error of at most 0.0051.
Values may be sent and summed in bfloat16 or wider, within the bound.
A program may use at most 512 MiB of HBM per device.

```python
import jax
import jax.numpy as jnp
from jax import lax

GROUPS = 128
GSIZE = 32
D = 4096
LAG = 8192
TOKENS = 4096


def steps_of(own_key, extent, shards, low, top_value):
    gain = 1.0
    for axis_at, blocks in shards:
        draws = jax.random.uniform(jax.random.fold_in(jax.random.fold_in(own_key, 6), axis_at), (blocks,), jnp.float32, low / len(shards), top_value / len(shards))
        gain = gain * jnp.repeat(jnp.exp(draws), extent[axis_at] // blocks).reshape((-1,) + (1,) * (len(extent) - 1 - axis_at))
    return gain


def scatter_about(own_key, extent, scale, most, split=(), kind=jnp.bfloat16):
    values = jax.random.normal(own_key, extent, jnp.float32) * scale
    if len(split) > 0:
        values = steps_of(own_key, extent, split, -0.22, 0.18) * values
    return jnp.clip(values, min=-most, max=most).astype(kind)


def setup_inputs(seed: int = 0) -> dict:
    arg_keys = jax.random.split(jax.random.key(seed), 5)
    return {
        "conv_input": scatter_about(arg_keys[0], (TOKENS, D), 0.0014, 0.0078125, ((0, 4), (1, 8))),
        "grad_out": scatter_about(arg_keys[1], (TOKENS, D), 1.0, 6.0, ((0, 32),)),
        "out_weight": scatter_about(arg_keys[2], (D, D), D ** -0.5, 0.09375, ((0, 8),)),
        "filters": scatter_about(arg_keys[3], (GROUPS, LAG), LAG ** -0.5, 0.0625, ((0, 8),)),
    }


def reference(conv_input, grad_out, out_weight, filters):
    grad_mid = jnp.dot(grad_out, out_weight.T, preferred_element_type=jnp.float32).astype(jnp.bfloat16)
    grad_mid = lax.optimization_barrier(grad_mid).astype(jnp.float32)
    inputs = conv_input.astype(jnp.float32)
    length = TOKENS + LAG
    grad_groups = grad_mid.reshape(TOKENS, GROUPS, GSIZE).transpose(1, 0, 2)
    input_groups = inputs.reshape(TOKENS, GROUPS, GSIZE).transpose(1, 0, 2)

    def per_group(items):
        grad_group, input_group, filter_group = items
        spec_grad = jnp.fft.rfft(grad_group, n=length, axis=0)
        spec_filter = jnp.fft.rfft(filter_group, n=length)
        spec_input = jnp.fft.rfft(input_group, n=length, axis=0)
        through = jnp.fft.irfft(spec_grad * jnp.conj(spec_filter)[:, None], n=length, axis=0)[:TOKENS]
        lagged = jnp.fft.irfft(jnp.sum(spec_grad * jnp.conj(spec_input), axis=1), n=length)[:LAG]
        return through, lagged

    through, lagged = lax.map(per_group, (grad_groups, input_groups, filters.astype(jnp.float32)))
    grad_input = through.transpose(1, 0, 2).reshape(TOKENS, D).astype(jnp.bfloat16)
    return grad_input, lagged.astype(jnp.float32)
```

```python
import functools

import jax
import jax.numpy as jnp
from jax import lax
from jax.experimental import pallas as pl
from jax.experimental.pallas import tpu as pltpu
from jax.sharding import PartitionSpec as P

HALF = 128
BLK = 2 * HALF
SUB = 8


def conv_kernel(width, gm_ref, x_ref, f_ref, gi_ref, gf_ref, toep, prod, gm_rows, x_cols):
    groups = f_ref.shape[0]
    rows = gm_ref.shape[1]
    lags = f_ref.shape[2]
    used = min(lags, rows)
    count = rows // BLK
    span = rows + HALF
    depth = count * width

    @pl.loop(0, groups)
    def _(g):
        first = pl.multiple_of(g * width, width)

        taps = f_ref[g, :, :used]
        pieces = [jnp.zeros((1, HALF), jnp.float32), taps]
        if used < rows:
            pieces.append(jnp.zeros((1, rows - used), jnp.float32))
        line = jnp.concatenate(pieces, axis=1)
        base = jnp.concatenate(
            [line] + [pltpu.roll(line, r, 1) for r in range(1, SUB)], axis=0
        )
        for k in range(0, HALF // SUB, 2):
            low = base if k == 0 else pltpu.roll(base, k * SUB, 1)
            high = pltpu.roll(base, (k + 1) * SUB, 1)
            both = jnp.concatenate([low, high], axis=0).astype(jnp.bfloat16)
            toep[k * SUB : (k + 2) * SUB, HALF:] = both[:, HALF:]
        toep[:, :HALF] = jnp.zeros((HALF, HALF), jnp.bfloat16)

        for a in range(count):
            gm_rows[a * width : (a + 1) * width, :] = gm_ref[
                pl.ds(first, width), a * BLK : (a + 1) * BLK
            ]
        gm_rows[depth:, :] = jnp.zeros((gm_rows.shape[0] - depth, BLK), jnp.bfloat16)
        x_rows = jnp.concatenate(
            [x_ref[pl.ds(first, width), a * BLK : (a + 1) * BLK] for a in range(count)], axis=0
        )
        x_cols[...] = x_rows.T

        step = min(4, count)
        total = None
        for j in range(0, count, step):
            m = (count - j) * width
            left = jnp.concatenate(
                [gm_rows[(j + q) * width : (j + q) * width + m, :] for q in range(step)], axis=1
            )
            right = jnp.concatenate(
                [
                    toep[:, HALF + j * BLK : HALF + (j + step) * BLK],
                    toep[:, j * BLK : (j + step) * BLK],
                ],
                axis=0,
            )
            part = lax.dot_general(
                left, right, (((1,), (1,)), ((), ())), preferred_element_type=jnp.float32
            )
            if total is None:
                total = part
            else:
                total = jnp.concatenate([total[:m] + part, total[m:]], axis=0)
        for a in range(count):
            gi_ref[pl.ds(first, width), a * BLK : (a + 1) * BLK] = total[
                a * width : (a + 1) * width
            ].astype(jnp.bfloat16)

        prod[:, :HALF] = jnp.zeros((HALF, HALF), jnp.float32)
        for j in range(count):
            k = min(depth, -(-((count - j) * width) // BLK) * BLK)
            part = jnp.dot(
                x_cols[:, :k],
                gm_rows[j * width : j * width + k, :],
                preferred_element_type=jnp.float32,
            )
            lo = j * BLK
            if j:
                prod[:, lo : lo + HALF] += part[HALF:, :HALF]
            prod[:, lo + HALF : lo + BLK] = part[:HALF, :HALF] + part[HALF:, HALF:]
            prod[:, lo + BLK : lo + BLK + HALF] = part[:HALF, HALF:]
        acc = prod[:SUB, :]
        for k in range(1, HALF // SUB):
            acc = acc + pltpu.roll(prod[k * SUB : (k + 1) * SUB, :], span - k * SUB, 1)
        out = acc[:1]
        for r in range(1, SUB):
            out = out + pltpu.roll(acc[r : r + 1], span - r, 1)
        gf_ref[g, :, :used] = out[:, HALF : HALF + used]
        if used < lags:
            gf_ref[g, :, used:] = jnp.zeros((1, lags - used), jnp.float32)


def conv_grads(gm_major, x_major, filter_rows):
    groups, lags = filter_rows.shape
    channels, rows = gm_major.shape
    width = channels // groups
    depth = rows // BLK * width
    grad_wide, filter_part = pl.pallas_call(
        functools.partial(conv_kernel, width),
        out_shape=(
            jax.ShapeDtypeStruct((channels, rows), jnp.bfloat16),
            jax.ShapeDtypeStruct((groups, 1, lags), jnp.float32),
        ),
        in_specs=[pl.BlockSpec(memory_space=pltpu.VMEM)] * 3,
        out_specs=(pl.BlockSpec(memory_space=pltpu.VMEM),) * 2,
        scratch_shapes=[
            pltpu.VMEM((HALF, rows + HALF), jnp.bfloat16),
            pltpu.VMEM((HALF, rows + HALF), jnp.float32),
            pltpu.VMEM((2 * depth, BLK), jnp.bfloat16),
            pltpu.VMEM((BLK, depth), jnp.bfloat16),
        ],
        compiler_params=pltpu.CompilerParams(vmem_limit_bytes=48 * 1024 * 1024),
    )(gm_major, x_major, filter_rows.astype(jnp.float32).reshape(groups, 1, lags))
    return grad_wide, filter_part.reshape(groups, lags)


def on_device(conv_input, grad_out, out_weight, filters):
    grad_major = lax.dot_general(
        out_weight,
        lax.all_gather(grad_out, "chan", axis=0, tiled=True),
        (((1,), (1,)), ((), ())),
        preferred_element_type=jnp.float32,
    ).astype(jnp.bfloat16)
    seq_count = lax.axis_size("seq")
    wide_input = lax.all_to_all(conv_input.T, "seq", split_axis=0, concat_axis=1, tiled=True)
    wide_grad = lax.all_to_all(grad_major, "seq", split_axis=0, concat_axis=1, tiled=True)
    local_groups = filters.shape[0] // seq_count
    own_filters = lax.dynamic_slice_in_dim(
        filters, lax.axis_index("seq") * local_groups, local_groups, 0
    )
    grad_wide, filter_part = conv_grads(wide_grad, wide_input, own_filters)
    grad_back = lax.all_to_all(grad_wide, "seq", split_axis=1, concat_axis=0, tiled=True)
    grad_filters = lax.all_to_all(filter_part, "seq", split_axis=1, concat_axis=0, tiled=True)
    return (grad_back.T, grad_filters)


def solution(mesh):
    in_specs = (P("seq", "chan"), P(("seq", "chan"), None), P("chan", None), P("chan", None))
    out_specs = (P("seq", "chan"), P("chan", "seq"))
    return jax.shard_map(
        on_device, mesh=mesh, in_specs=in_specs, out_specs=out_specs, check_vma=False
    )
```

```python
import functools

import jax
import jax.numpy as jnp
from jax import lax
from jax.experimental import pallas as pl
from jax.experimental.pallas import tpu as pltpu
from jax.sharding import PartitionSpec as P

HALF = 128
BLK = 2 * HALF
SUB = 8

MESH = pl.DeviceIdType.MESH
PARTS = 2


def whole_kernel(
    chan_count, seq_count, width,
    x_hbm, go_hbm, w_hbm, f_ref,
    gi_out, gf_out,
    gath, w_vm, x_vm, x_turn, x_major, taps, toep, x_cols, gm_send, gm_wide, gm_rows,
    gi_send, gi_back, prod, gf_send, gf_back,
    load_sem, hop_send, hop_recv, x_send, x_recv, gm_ssem, gm_rsem, gi_ssem, gi_rsem, gf_ssem, gf_rsem,
):
    chips = chan_count // 2
    seq = lax.axis_index("seq")
    chan = lax.axis_index("chan")
    spot = chan // 2
    core = lax.rem(chan, 2)
    tok = go_hbm.shape[0]
    piece = tok // PARTS
    span_t = x_hbm.shape[0]
    rows = span_t * seq_count
    groups = f_ref.shape[0] // seq_count
    lags = f_ref.shape[1]
    used = min(lags, rows)
    own_ch = groups * width
    unit = 2 * tok
    count = rows // BLK
    span = rows + HALF
    depth = count * width
    cut = lags // seq_count

    up = {"chan": chan + 2}
    down = {"chan": chan - 2}
    twin = {"chan": chan + 1 - 2 * core}
    has_up = spot < chips - 1
    has_down = spot > 0

    def peer(r):
        return lax.rem(seq + r, seq_count)

    barrier = pltpu.get_barrier_semaphore()
    pl.semaphore_signal(barrier, inc=1, device_id=twin, device_id_type=MESH)
    for r in range(1, seq_count):
        pl.semaphore_signal(barrier, inc=1, device_id={"seq": peer(r)}, device_id_type=MESH)

    @pl.when(has_up)
    def _():
        pl.semaphore_signal(barrier, inc=1, device_id=up, device_id_type=MESH)

    @pl.when(has_down)
    def _():
        pl.semaphore_signal(barrier, inc=1, device_id=down, device_id_type=MESH)

    load_own = pltpu.make_async_copy(
        go_hbm, gath.at[spot, pl.ds(core * tok, tok)], load_sem.at[0]
    )
    load_own.start()
    load_x = pltpu.make_async_copy(x_hbm, x_vm, load_sem.at[1])
    load_x.start()
    load_w = pltpu.make_async_copy(w_hbm, w_vm, load_sem.at[2])
    load_w.start()

    @pl.when(has_up & has_down)
    def _():
        pl.semaphore_wait(barrier, seq_count + 2)

    @pl.when(jnp.logical_not(has_up & has_down))
    def _():
        pl.semaphore_wait(barrier, seq_count + min(chips - 1, 1))

    def slot(q, side, h):
        return gath.at[q, pl.ds(pl.multiple_of(side * tok + h * piece, piece), piece)]

    def hop(way, q, h, target):
        return pltpu.make_async_remote_copy(
            src_ref=slot(q, core, h),
            dst_ref=slot(q, core, h),
            send_sem=hop_send.at[way, q, h],
            recv_sem=hop_recv.at[q, core, h],
            device_id=target,
            device_id_type=MESH,
        )

    def arrived(q, side, h):
        pltpu.make_async_remote_copy(
            src_ref=slot(q, side, h),
            dst_ref=slot(q, side, h),
            send_sem=hop_send.at[2, q, h],
            recv_sem=hop_recv.at[q, side, h],
            device_id=twin,
            device_id_type=MESH,
        ).wait_recv()

    load_own.wait()
    for h in range(PARTS):
        @pl.when(has_up)
        def _():
            hop(0, spot, h, up).start()

        @pl.when(has_down)
        def _():
            hop(1, spot, h, down).start()

    for h in range(PARTS):
        hop(2, spot, h, twin).start()

    load_x.wait()
    for i in range(0, x_vm.shape[1], HALF):
        x_turn[i : i + HALF, :] = x_vm[:, i : i + HALF].T

    def x_copy(source, target):
        return pltpu.make_async_remote_copy(
            src_ref=x_turn.at[pl.ds(pl.multiple_of(target * own_ch, own_ch), own_ch)],
            dst_ref=x_major.at[source],
            send_sem=x_send.at[target],
            recv_sem=x_recv.at[source],
            device_id={"seq": target},
            device_id_type=MESH,
        )

    for r in range(1, seq_count):
        x_copy(seq, peer(r)).start()
    x_major[seq] = x_turn[pl.ds(pl.multiple_of(seq * own_ch, own_ch), own_ch), :]

    for i in range(f_ref.shape[0]):
        taps[i] = f_ref[i : i + 1, :used].astype(jnp.float32)

    @pl.loop(0, groups)
    def _(g):
        pieces = [jnp.zeros((1, HALF), jnp.float32), taps[seq * groups + g]]
        if used < rows:
            pieces.append(jnp.zeros((1, rows - used), jnp.float32))
        line = jnp.concatenate(pieces, axis=1)
        base = jnp.concatenate(
            [line] + [pltpu.roll(line, r, 1) for r in range(1, SUB)], axis=0
        )
        for k in range(0, HALF // SUB, 2):
            low = base if k == 0 else pltpu.roll(base, k * SUB, 1)
            high = pltpu.roll(base, (k + 1) * SUB, 1)
            both = jnp.concatenate([low, high], axis=0).astype(jnp.bfloat16)
            toep[g, k * SUB : (k + 2) * SUB, HALF:] = both[:, HALF:]
        toep[g, :, :HALF] = jnp.zeros((HALF, HALF), jnp.bfloat16)

    def gm_copy(q, source, target):
        return pltpu.make_async_remote_copy(
            src_ref=gm_send.at[q, pl.ds(pl.multiple_of(target * own_ch, own_ch), own_ch)],
            dst_ref=gm_wide.at[source * chips + q],
            send_sem=gm_ssem.at[q, target],
            recv_sem=gm_rsem.at[q, source],
            device_id={"seq": target},
            device_id_type=MESH,
        )

    def project(q):
        for h in range(PARTS):
            arrived(q, 1 - core, h)
        gm_send[q] = lax.dot_general(
            w_vm[...], gath[q], (((1,), (1,)), ((), ())), preferred_element_type=jnp.float32
        ).astype(jnp.bfloat16)
        for r in range(1, seq_count):
            gm_copy(q, seq, peer(r)).start()
        gm_wide[seq * chips + q] = gm_send[
            q, pl.ds(pl.multiple_of(seq * own_ch, own_ch), own_ch), :
        ]

    load_w.wait()
    for r in range(1, seq_count):
        x_copy(peer(r), seq).wait_recv()

    @pl.loop(0, groups)
    def _(g):
        first = pl.multiple_of(g * width, width)
        per = span_t // BLK
        x_rows = jnp.concatenate(
            [
                x_major[a // per, pl.ds(first, width), (a % per) * BLK : (a % per + 1) * BLK]
                for a in range(count)
            ],
            axis=0,
        )
        x_cols[g] = x_rows.T

    def relay(d):
        for h in range(PARTS):
            @pl.when(spot >= d)
            def _():
                arrived(spot - d, core, h)

                @pl.when(has_up)
                def _():
                    hop(0, spot - d, h, up).start()

                hop(2, spot - d, h, twin).start()

            @pl.when(spot + d < chips)
            def _():
                arrived(spot + d, core, h)

                @pl.when(has_down)
                def _():
                    hop(1, spot + d, h, down).start()

                hop(2, spot + d, h, twin).start()

    @pl.loop(0, chips)
    def _(d):
        @pl.when(d > 0)
        def _():
            relay(d)

        @pl.loop(0, 2)
        def _(side):
            q = spot - d + 2 * d * side

            @pl.when((q >= 0) & (q < chips) & (d + 1 - side > 0))
            def _():
                project(q)

    @pl.loop(0, chips)
    def _(q):
        for r in range(1, seq_count):
            gm_copy(q, peer(r), seq).wait_recv()

    def gi_copy(g, source, target):
        return pltpu.make_async_remote_copy(
            src_ref=gi_send.at[target, g],
            dst_ref=gi_back.at[source, g],
            send_sem=gi_ssem.at[g, target],
            recv_sem=gi_rsem.at[g, source],
            device_id={"seq": target},
            device_id_type=MESH,
        )

    def gf_copy(source, target):
        return pltpu.make_async_remote_copy(
            src_ref=gf_send.at[target],
            dst_ref=gf_back.at[source],
            send_sem=gf_ssem.at[target],
            recv_sem=gf_rsem.at[source],
            device_id={"seq": target},
            device_id_type=MESH,
        )

    @pl.loop(0, groups)
    def _(g):
        first = pl.multiple_of(g * width, width)
        fold = BLK // unit
        for a in range(count):
            for u in range(fold):
                gm_rows[a * width : (a + 1) * width, u * unit : (u + 1) * unit] = gm_wide[
                    a * fold + u, pl.ds(first, width), :
                ]
        gm_rows[depth:, :] = jnp.zeros((gm_rows.shape[0] - depth, BLK), jnp.bfloat16)

        step = min(4, count)
        total = None
        for j in range(0, count, step):
            m = (count - j) * width
            left = jnp.concatenate(
                [gm_rows[(j + q) * width : (j + q) * width + m, :] for q in range(step)], axis=1
            )
            right = jnp.concatenate(
                [
                    toep[g, :, HALF + j * BLK : HALF + (j + step) * BLK],
                    toep[g, :, j * BLK : (j + step) * BLK],
                ],
                axis=0,
            )
            part = lax.dot_general(
                left, right, (((1,), (1,)), ((), ())), preferred_element_type=jnp.float32
            )
            if total is None:
                total = part
            else:
                total = jnp.concatenate([total[:m] + part, total[m:]], axis=0)
        per = span_t // BLK
        for a in range(count):
            gi_send[a // per, g, :, (a % per) * BLK : (a % per + 1) * BLK] = total[
                a * width : (a + 1) * width
            ].astype(jnp.bfloat16)
        for r in range(1, seq_count):
            gi_copy(g, seq, peer(r)).start()
        gi_back[seq, g] = gi_send[seq, g]

        prod[:, :HALF] = jnp.zeros((HALF, HALF), jnp.float32)
        for j in range(count):
            k = min(depth, -(-((count - j) * width) // BLK) * BLK)
            part = jnp.dot(
                x_cols[g, :, :k],
                gm_rows[j * width : j * width + k, :],
                preferred_element_type=jnp.float32,
            )
            lo = j * BLK
            if j:
                prod[:, lo : lo + HALF] += part[HALF:, :HALF]
            prod[:, lo + HALF : lo + BLK] = part[:HALF, :HALF] + part[HALF:, HALF:]
            prod[:, lo + BLK : lo + BLK + HALF] = part[:HALF, HALF:]
        acc = prod[:SUB, :]
        for k in range(1, HALF // SUB):
            acc = acc + pltpu.roll(prod[k * SUB : (k + 1) * SUB, :], span - k * SUB, 1)
        out = acc[:1]
        for r in range(1, SUB):
            out = out + pltpu.roll(acc[r : r + 1], span - r, 1)
        for s in range(seq_count):
            live = min(max(used - s * cut, 0), cut)
            if live:
                gf_send[s, g, :, :live] = out[:, HALF + s * cut : HALF + s * cut + live]
            if live < cut:
                gf_send[s, g, :, live:] = jnp.zeros((1, cut - live), jnp.float32)

    for r in range(1, seq_count):
        gf_copy(seq, peer(r)).start()
    gf_back[seq] = gf_send[seq]

    @pl.loop(0, groups)
    def _(g):
        for r in range(1, seq_count):
            gi_copy(g, peer(r), seq).wait_recv()

    per_tile = max(1, HALF // own_ch)
    for s in range(0, seq_count, per_tile):
        tile = jnp.concatenate(
            [gi_back[s + i, g] for i in range(per_tile) for g in range(groups)], axis=0
        )
        gi_out[:, s * own_ch : (s + per_tile) * own_ch] = tile.T
    for r in range(1, seq_count):
        gf_copy(peer(r), seq).wait_recv()
    for s in range(seq_count):
        for g in range(groups):
            gf_out[s * groups + g : s * groups + g + 1, :] = gf_back[s, g]

    for r in range(1, seq_count):
        x_copy(seq, peer(r)).wait_send()
        gf_copy(seq, peer(r)).wait_send()

    @pl.loop(0, groups)
    def _(g):
        for r in range(1, seq_count):
            gi_copy(g, seq, peer(r)).wait_send()

    @pl.loop(0, chips)
    def _(q):
        for r in range(1, seq_count):
            gm_copy(q, seq, peer(r)).wait_send()
        for h in range(PARTS):
            hop(2, q, h, twin).wait_send()

            @pl.when(has_up & (q <= spot))
            def _():
                hop(0, q, h, up).wait_send()

            @pl.when(has_down & (q >= spot))
            def _():
                hop(1, q, h, down).wait_send()


def on_device(chan_count, seq_count, conv_input, grad_out, out_weight, filters):
    span_t, chans = conv_input.shape
    tok, model = grad_out.shape
    all_groups, lags = filters.shape
    width = chans // all_groups
    groups = all_groups // seq_count
    own_ch = groups * width
    rows = span_t * seq_count
    chips = chan_count // 2
    unit = 2 * tok
    count = rows // BLK
    depth = count * width
    cut = lags // seq_count
    used = min(lags, rows)
    bf16, f32 = jnp.bfloat16, jnp.float32
    dma = pltpu.SemaphoreType.DMA
    hbm = pl.BlockSpec(memory_space=pl.ANY)
    vmem = pl.BlockSpec(memory_space=pltpu.VMEM)
    work = chans * rows * model // seq_count + 2 * own_ch * rows * rows
    return pl.pallas_call(
        functools.partial(whole_kernel, chan_count, seq_count, width),
        out_shape=(
            jax.ShapeDtypeStruct((span_t, chans), bf16),
            jax.ShapeDtypeStruct((all_groups, cut), f32),
        ),
        in_specs=[hbm, hbm, hbm, vmem],
        out_specs=(vmem, vmem),
        scratch_shapes=[
            pltpu.VMEM((chips, unit, model), bf16),
            pltpu.VMEM(out_weight.shape, bf16),
            pltpu.VMEM((span_t, chans), bf16),
            pltpu.VMEM((chans, span_t), bf16),
            pltpu.VMEM((seq_count, own_ch, span_t), bf16),
            pltpu.VMEM((all_groups, 1, used), f32),
            pltpu.VMEM((groups, HALF, rows + HALF), bf16),
            pltpu.VMEM((groups, BLK, depth), bf16),
            pltpu.VMEM((chips, chans, unit), bf16),
            pltpu.VMEM((seq_count * chips, own_ch, unit), bf16),
            pltpu.VMEM((2 * depth, BLK), bf16),
            pltpu.VMEM((seq_count, groups, width, span_t), bf16),
            pltpu.VMEM((seq_count, groups, width, span_t), bf16),
            pltpu.VMEM((HALF, rows + HALF), f32),
            pltpu.VMEM((seq_count, groups, 1, cut), f32),
            pltpu.VMEM((seq_count, groups, 1, cut), f32),
            dma((3,)),
            dma((3, chips, PARTS)),
            dma((chips, 2, PARTS)),
            dma((seq_count,)),
            dma((seq_count,)),
            dma((chips, seq_count)),
            dma((chips, seq_count)),
            dma((groups, seq_count)),
            dma((groups, seq_count)),
            dma((seq_count,)),
            dma((seq_count,)),
        ],
        cost_estimate=pl.CostEstimate(
            flops=2 * work, bytes_accessed=16 * 1024 * 1024, transcendentals=0
        ),
        compiler_params=pltpu.CompilerParams(
            vmem_limit_bytes=56 * 1024 * 1024, collective_id=0, has_side_effects=True
        ),
    )(conv_input, grad_out, out_weight, filters)


def solution(mesh):
    in_specs = (P("seq", "chan"), P(("seq", "chan"), None), P("chan", None), P("chan", None))
    out_specs = (P("seq", "chan"), P("chan", "seq"))
    return jax.shard_map(
        functools.partial(on_device, mesh.shape["chan"], mesh.shape["seq"]),
        mesh=mesh, in_specs=in_specs, out_specs=out_specs, check_vma=False,
    )
```

```python
import functools

import jax
import jax.numpy as jnp
from jax import lax
from jax.experimental import pallas as pl
from jax.experimental.pallas import tpu as pltpu
from jax.sharding import PartitionSpec as P

HALF = 128
BLK = 2 * HALF
SUB = 8

MESH = pl.DeviceIdType.MESH
PARTS = 4


def whole_kernel(
    chan_count, seq_count, width,
    x_hbm, go_hbm, w_hbm, f_ref,
    gi_out, gf_out,
    gath, w_vm, x_vm, x_turn, x_major, taps, toep, x_cols, gm_send, gm_wide, gm_rows,
    gi_send, prod, gf_send, w_far, gm_far,
    far_ssem, far_psem, far_rsem, far_gsem, own_sem, load_sem, hop_send, hop_recv, x_send, x_recv, gm_ssem, gm_rsem, gi_ssem, gi_rsem, gf_ssem, gf_rsem,
):
    chips = chan_count // 2
    seq = lax.axis_index("seq")
    chan = lax.axis_index("chan")
    spot = chan // 2
    core = lax.rem(chan, 2)
    tok = go_hbm.shape[0]
    piece = tok // PARTS
    span_t = x_hbm.shape[0]
    rows = span_t * seq_count
    groups = f_ref.shape[0] // seq_count
    lags = f_ref.shape[1]
    used = min(lags, rows)
    own_ch = groups * width
    unit = 2 * tok
    count = rows // BLK
    span = rows + HALF
    depth = count * width
    cut = lags // seq_count

    up = {"chan": chan + 2}
    down = {"chan": chan - 2}
    twin = {"chan": chan + 1 - 2 * core}
    has_up = spot < chips - 1
    has_down = spot > 0

    upper = (2 * spot) // chips
    edge = spot + upper * (chips - 1 - 2 * spot)
    is_end = edge == 0 if chips >= 4 else spot < 0
    is_inner = edge == 1 if chips >= 4 else spot < 0
    mate = chan + (1 - 2 * upper) * (2 - 4 * edge)
    far = (1 - upper) * (chips - 1)
    far_parts = min(PARTS, own_ch // 16)
    far_rows = own_ch // far_parts

    def held(q):
        return jnp.logical_not(is_end & (q == far))

    def onward(q):
        return jnp.logical_not(is_inner & (q == far))

    def peer(r):
        return lax.rem(seq + r, seq_count)

    barrier = pltpu.get_barrier_semaphore()
    pl.semaphore_signal(barrier, inc=1, device_id=twin, device_id_type=MESH)
    for r in range(1, seq_count):
        pl.semaphore_signal(barrier, inc=1, device_id={"seq": peer(r)}, device_id_type=MESH)

    @pl.when(has_up)
    def _():
        pl.semaphore_signal(barrier, inc=1, device_id=up, device_id_type=MESH)

    @pl.when(has_down)
    def _():
        pl.semaphore_signal(barrier, inc=1, device_id=down, device_id_type=MESH)

    @pl.when(is_end | is_inner)
    def _():
        for r in range(1, seq_count):
            pl.semaphore_signal(
                barrier, inc=1, device_id={"seq": peer(r), "chan": mate}, device_id_type=MESH
            )

    load_own = pltpu.make_async_copy(
        go_hbm, gath.at[spot, pl.ds(core * tok, tok)], load_sem.at[0]
    )
    load_own.start()
    load_x = pltpu.make_async_copy(x_hbm, x_vm, load_sem.at[1])
    load_x.start()
    load_w = pltpu.make_async_copy(w_hbm, w_vm, load_sem.at[2])
    load_w.start()

    greeted = seq_count - 1 if chips >= 4 else 0

    @pl.when((edge == 1) & has_up & has_down)
    def _():
        pl.semaphore_wait(barrier, seq_count + 2 + greeted)

    @pl.when((edge > 1) & has_up & has_down)
    def _():
        pl.semaphore_wait(barrier, seq_count + 2)

    @pl.when(jnp.logical_not(has_up & has_down))
    def _():
        pl.semaphore_wait(barrier, seq_count + min(chips - 1, 1) + greeted)

    def slot(q, side, h):
        return gath.at[q, pl.ds(pl.multiple_of(side * tok + h * piece, piece), piece)]

    def hop(way, q, h, target):
        return pltpu.make_async_remote_copy(
            src_ref=slot(q, core, h),
            dst_ref=slot(q, core, h),
            send_sem=hop_send.at[way, q, h],
            recv_sem=hop_recv.at[q, core, h],
            device_id=target,
            device_id_type=MESH,
        )

    def arrived(q, side, h):
        pltpu.make_async_remote_copy(
            src_ref=slot(q, side, h),
            dst_ref=slot(q, side, h),
            send_sem=hop_send.at[2, q, h],
            recv_sem=hop_recv.at[q, side, h],
            device_id=twin,
            device_id_type=MESH,
        ).wait_recv()

    def far_span(s, h):
        return pl.ds(pl.multiple_of(s * own_ch + h * far_rows, far_rows), far_rows)

    def far_hop(h):
        return pltpu.make_async_remote_copy(
            src_ref=w_hbm.at[far_span(seq, h)],
            dst_ref=w_far.at[far_span(seq, h)],
            send_sem=far_ssem.at[h],
            recv_sem=far_rsem.at[seq, h],
            device_id={"chan": mate},
            device_id_type=MESH,
        )

    def far_share(source, target, h):
        return pltpu.make_async_remote_copy(
            src_ref=w_far.at[far_span(source, h)],
            dst_ref=w_far.at[far_span(source, h)],
            send_sem=far_psem.at[target, h],
            recv_sem=far_rsem.at[source, h],
            device_id={"seq": target},
            device_id_type=MESH,
        )

    def far_gm(source, target):
        return pltpu.make_async_remote_copy(
            src_ref=gm_far.at[pl.ds(pl.multiple_of(target * own_ch, own_ch), own_ch)],
            dst_ref=gm_wide.at[source * chips + far],
            send_sem=far_gsem.at[target],
            recv_sem=gm_rsem.at[far, source],
            device_id={"seq": target, "chan": mate},
            device_id_type=MESH,
        )

    load_own.wait()
    for h in range(PARTS):
        @pl.when(has_up)
        def _():
            hop(0, spot, h, up).start()

        @pl.when(has_down)
        def _():
            hop(1, spot, h, down).start()

        if h < far_parts:
            @pl.when(is_end)
            def _():
                far_hop(h).start()

    for h in range(PARTS):
        hop(2, spot, h, twin).start()

    load_x.wait()
    for i in range(0, x_vm.shape[1], HALF):
        x_turn[i : i + HALF, :] = x_vm[:, i : i + HALF].T

    def x_copy(source, target):
        return pltpu.make_async_remote_copy(
            src_ref=x_turn.at[pl.ds(pl.multiple_of(target * own_ch, own_ch), own_ch)],
            dst_ref=x_major.at[source],
            send_sem=x_send.at[target],
            recv_sem=x_recv.at[source],
            device_id={"seq": target},
            device_id_type=MESH,
        )

    for r in range(1, seq_count):
        x_copy(seq, peer(r)).start()
    x_major[seq] = x_turn[pl.ds(pl.multiple_of(seq * own_ch, own_ch), own_ch), :]

    for i in range(f_ref.shape[0]):
        taps[i] = f_ref[i : i + 1, :used].astype(jnp.float32)

    @pl.loop(0, groups)
    def _(g):
        pieces = [jnp.zeros((1, HALF), jnp.float32), taps[seq * groups + g]]
        if used < rows:
            pieces.append(jnp.zeros((1, rows - used), jnp.float32))
        line = jnp.concatenate(pieces, axis=1)
        base = jnp.concatenate(
            [line] + [pltpu.roll(line, r, 1) for r in range(1, SUB)], axis=0
        )
        for k in range(0, HALF // SUB, 2):
            low = base if k == 0 else pltpu.roll(base, k * SUB, 1)
            high = pltpu.roll(base, (k + 1) * SUB, 1)
            both = jnp.concatenate([low, high], axis=0).astype(jnp.bfloat16)
            toep[g, k * SUB : (k + 2) * SUB, HALF:] = both[:, HALF:]
        toep[g, :, :HALF] = jnp.zeros((HALF, HALF), jnp.bfloat16)

    def gm_copy(q, source, target):
        return pltpu.make_async_remote_copy(
            src_ref=gm_send.at[q, pl.ds(pl.multiple_of(target * own_ch, own_ch), own_ch)],
            dst_ref=gm_wide.at[source * chips + q],
            send_sem=gm_ssem.at[q, target],
            recv_sem=gm_rsem.at[q, source],
            device_id={"seq": target},
            device_id_type=MESH,
        )

    def project_far():
        for r in range(1, seq_count):
            for h in range(far_parts):
                far_share(peer(r), seq, h).wait_recv()
        gm_far[...] = lax.dot_general(
            w_far[...], gath[far], (((1,), (1,)), ((), ())), preferred_element_type=jnp.float32
        ).astype(jnp.bfloat16)
        for r in range(seq_count):
            far_gm(seq, peer(r)).start()

    def project(q):
        gm_send[q] = lax.dot_general(
            w_vm[...], gath[q], (((1,), (1,)), ((), ())), preferred_element_type=jnp.float32
        ).astype(jnp.bfloat16)
        for r in range(1, seq_count):
            gm_copy(q, seq, peer(r)).start()
        gm_wide[seq * chips + q] = gm_send[
            q, pl.ds(pl.multiple_of(seq * own_ch, own_ch), own_ch), :
        ]

    load_w.wait()
    for r in range(1, seq_count):
        x_copy(peer(r), seq).wait_recv()

    @pl.loop(0, groups)
    def _(g):
        first = pl.multiple_of(g * width, width)
        per = span_t // BLK
        x_rows = jnp.concatenate(
            [
                x_major[a // per, pl.ds(first, width), (a % per) * BLK : (a % per + 1) * BLK]
                for a in range(count)
            ],
            axis=0,
        )
        x_cols[g] = x_rows.T

    def relay(d):
        for h in range(PARTS):
            @pl.when((spot >= d) & held(spot - d))
            def _():
                arrived(spot - d, core, h)

                @pl.when(has_up & onward(spot - d))
                def _():
                    hop(0, spot - d, h, up).start()

                hop(2, spot - d, h, twin).start()

            @pl.when((spot + d < chips) & held(spot + d))
            def _():
                arrived(spot + d, core, h)

                @pl.when(has_down & onward(spot + d))
                def _():
                    hop(1, spot + d, h, down).start()

                hop(2, spot + d, h, twin).start()

            if h < far_parts:
                @pl.when(is_inner & (d == 1))
                def _():
                    far_hop(h).wait_recv()
                    for r in range(1, seq_count):
                        far_share(seq, peer(r), h).start()

    @pl.loop(0, chips)
    def _(d):
        @pl.when(d > 0)
        def _():
            relay(d)

        @pl.loop(0, 2)
        def _(side):
            q = spot - d + 2 * d * side

            @pl.when((q >= 0) & (q < chips) & (d + 1 - side > 0) & held(q))
            def _():
                for h in range(PARTS):
                    arrived(q, 1 - core, h)

                @pl.when(is_inner & (q == far))
                def _():
                    project_far()

                project(q)

    @pl.loop(0, chips)
    def _(q):
        for r in range(1, seq_count):
            gm_copy(q, peer(r), seq).wait_recv()

        @pl.when(is_end & (q == far))
        def _():
            far_gm(seq, seq).wait_recv()

    def gi_copy(g, source, target):
        return pltpu.make_async_remote_copy(
            src_ref=gi_send.at[target, g],
            dst_ref=gi_out.at[source, g],
            send_sem=gi_ssem.at[g, target],
            recv_sem=gi_rsem.at[g, source],
            device_id={"seq": target},
            device_id_type=MESH,
        )

    def gf_copy(source, target):
        return pltpu.make_async_remote_copy(
            src_ref=gf_send.at[target],
            dst_ref=gf_out.at[source],
            send_sem=gf_ssem.at[target],
            recv_sem=gf_rsem.at[source],
            device_id={"seq": target},
            device_id_type=MESH,
        )

    @pl.loop(0, groups)
    def _(g):
        first = pl.multiple_of(g * width, width)
        fold = BLK // unit
        for a in range(count):
            for u in range(fold):
                gm_rows[g, a * width : (a + 1) * width, u * unit : (u + 1) * unit] = gm_wide[
                    a * fold + u, pl.ds(first, width), :
                ]
        gm_rows[g, depth:, :] = jnp.zeros((depth, BLK), jnp.bfloat16)

        step = min(4, count)
        total = None
        for j in range(0, count, step):
            m = (count - j) * width
            left = jnp.concatenate(
                [gm_rows[g, (j + q) * width : (j + q) * width + m, :] for q in range(step)], axis=1
            )
            right = jnp.concatenate(
                [
                    toep[g, :, HALF + j * BLK : HALF + (j + step) * BLK],
                    toep[g, :, j * BLK : (j + step) * BLK],
                ],
                axis=0,
            )
            part = lax.dot_general(
                left, right, (((1,), (1,)), ((), ())), preferred_element_type=jnp.float32
            )
            if total is None:
                total = part
            else:
                total = jnp.concatenate([total[:m] + part, total[m:]], axis=0)
        per = span_t // BLK
        for a in range(count):
            gi_send[a // per, g, :, (a % per) * BLK : (a % per + 1) * BLK] = total[
                a * width : (a + 1) * width
            ].astype(jnp.bfloat16)
        for r in range(1, seq_count):
            gi_copy(g, seq, peer(r)).start()
        pltpu.make_async_copy(gi_send.at[seq, g], gi_out.at[seq, g], own_sem.at[g]).start()

    @pl.loop(0, groups)
    def _(g):

        prod[:, :HALF] = jnp.zeros((HALF, HALF), jnp.float32)
        for j in range(count):
            k = min(depth, -(-((count - j) * width) // BLK) * BLK)
            part = jnp.dot(
                x_cols[g, :, :k],
                gm_rows[g, j * width : j * width + k, :],
                preferred_element_type=jnp.float32,
            )
            lo = j * BLK
            if j:
                prod[:, lo : lo + HALF] += part[HALF:, :HALF]
            prod[:, lo + HALF : lo + BLK] = part[:HALF, :HALF] + part[HALF:, HALF:]
            prod[:, lo + BLK : lo + BLK + HALF] = part[:HALF, HALF:]
        acc = prod[:SUB, :]
        for k in range(1, HALF // SUB):
            acc = acc + pltpu.roll(prod[k * SUB : (k + 1) * SUB, :], span - k * SUB, 1)
        out = acc[:1]
        for r in range(1, SUB):
            out = out + pltpu.roll(acc[r : r + 1], span - r, 1)
        for s in range(seq_count):
            live = min(max(used - s * cut, 0), cut)
            if live:
                gf_send[s, g, :, :live] = out[:, HALF + s * cut : HALF + s * cut + live]
            if live < cut:
                gf_send[s, g, :, live:] = jnp.zeros((1, cut - live), jnp.float32)

    for r in range(1, seq_count):
        gf_copy(seq, peer(r)).start()
    own_gf = pltpu.make_async_copy(gf_send.at[seq], gf_out.at[seq], own_sem.at[groups])
    own_gf.start()

    @pl.loop(0, groups)
    def _(g):
        for r in range(1, seq_count):
            gi_copy(g, peer(r), seq).wait_recv()

    for r in range(1, seq_count):
        gf_copy(peer(r), seq).wait_recv()
    own_gf.wait()

    for r in range(1, seq_count):
        x_copy(seq, peer(r)).wait_send()
        gf_copy(seq, peer(r)).wait_send()

    @pl.loop(0, groups)
    def _(g):
        for r in range(1, seq_count):
            gi_copy(g, seq, peer(r)).wait_send()
        pltpu.make_async_copy(gi_send.at[seq, g], gi_out.at[seq, g], own_sem.at[g]).wait()

    @pl.loop(0, chips)
    def _(q):
        @pl.when(held(q))
        def _():
            for r in range(1, seq_count):
                gm_copy(q, seq, peer(r)).wait_send()
            for h in range(PARTS):
                hop(2, q, h, twin).wait_send()

        for h in range(PARTS):
            @pl.when(has_up & (q <= spot) & held(q) & onward(q))
            def _():
                hop(0, q, h, up).wait_send()

            @pl.when(has_down & (q >= spot) & held(q) & onward(q))
            def _():
                hop(1, q, h, down).wait_send()

    @pl.when(is_end)
    def _():
        for h in range(far_parts):
            far_hop(h).wait_send()

    @pl.when(is_inner)
    def _():
        for r in range(1, seq_count):
            for h in range(far_parts):
                far_share(seq, peer(r), h).wait_send()
        for r in range(seq_count):
            far_gm(seq, peer(r)).wait_send()


def on_device(chan_count, seq_count, conv_input, grad_out, out_weight, filters):
    span_t, chans = conv_input.shape
    tok, model = grad_out.shape
    all_groups, lags = filters.shape
    width = chans // all_groups
    groups = all_groups // seq_count
    own_ch = groups * width
    rows = span_t * seq_count
    chips = chan_count // 2
    unit = 2 * tok
    count = rows // BLK
    depth = count * width
    cut = lags // seq_count
    used = min(lags, rows)
    bf16, f32 = jnp.bfloat16, jnp.float32
    dma = pltpu.SemaphoreType.DMA
    hbm = pl.BlockSpec(memory_space=pl.ANY)
    vmem = pl.BlockSpec(memory_space=pltpu.VMEM)
    work = chans * rows * model // seq_count + 2 * own_ch * rows * rows
    through, lagged = pl.pallas_call(
        functools.partial(whole_kernel, chan_count, seq_count, width),
        out_shape=(
            jax.ShapeDtypeStruct((seq_count, groups, width, span_t), bf16),
            jax.ShapeDtypeStruct((seq_count, groups, 1, cut), f32),
        ),
        in_specs=[hbm, hbm, hbm, vmem],
        out_specs=(hbm, hbm),
        scratch_shapes=[
            pltpu.VMEM((chips, unit, model), bf16),
            pltpu.VMEM(out_weight.shape, bf16),
            pltpu.VMEM((span_t, chans), bf16),
            pltpu.VMEM((chans, span_t), bf16),
            pltpu.VMEM((seq_count, own_ch, span_t), bf16),
            pltpu.VMEM((all_groups, 1, used), f32),
            pltpu.VMEM((groups, HALF, rows + HALF), bf16),
            pltpu.VMEM((groups, BLK, depth), bf16),
            pltpu.VMEM((chips, chans, unit), bf16),
            pltpu.VMEM((seq_count * chips, own_ch, unit), bf16),
            pltpu.VMEM((groups, 2 * depth, BLK), bf16),
            pltpu.VMEM((seq_count, groups, width, span_t), bf16),
            pltpu.VMEM((HALF, rows + HALF), f32),
            pltpu.VMEM((seq_count, groups, 1, cut), f32),
            pltpu.VMEM(out_weight.shape, bf16),
            pltpu.VMEM((chans, unit), bf16),
            dma((PARTS,)),
            dma((seq_count, PARTS)),
            dma((seq_count, PARTS)),
            dma((seq_count,)),
            dma((groups + 1,)),
            dma((3,)),
            dma((3, chips, PARTS)),
            dma((chips, 2, PARTS)),
            dma((seq_count,)),
            dma((seq_count,)),
            dma((chips, seq_count)),
            dma((chips, seq_count)),
            dma((groups, seq_count)),
            dma((groups, seq_count)),
            dma((seq_count,)),
            dma((seq_count,)),
        ],
        cost_estimate=pl.CostEstimate(
            flops=2 * work, bytes_accessed=16 * 1024 * 1024, transcendentals=0
        ),
        compiler_params=pltpu.CompilerParams(
            vmem_limit_bytes=56 * 1024 * 1024, collective_id=0, has_side_effects=True
        ),
    )(conv_input, grad_out, out_weight, filters)
    return through.reshape(chans, span_t).T, lagged.reshape(all_groups, cut)


def solution(mesh):
    in_specs = (P("seq", "chan"), P(("seq", "chan"), None), P("chan", None), P("chan", None))
    out_specs = (P("seq", "chan"), P("chan", "seq"))
    return jax.shard_map(
        functools.partial(on_device, mesh.shape["chan"], mesh.shape["seq"]),
        mesh=mesh, in_specs=in_specs, out_specs=out_specs, check_vma=False,
    )
```

```python
import functools

import jax
import jax.numpy as jnp
from jax import lax
from jax.experimental import pallas as pl
from jax.experimental.pallas import tpu as pltpu
from jax.sharding import PartitionSpec as P

HALF = 128
BLK = 2 * HALF
SUB = 8

MESH = pl.DeviceIdType.MESH
PARTS = 4


def whole_kernel(
    chan_count, seq_count, width,
    x_hbm, go_hbm, w_hbm, f_ref,
    gi_out, gf_out,
    gath, w_vm, x_vm, x_turn, x_major, taps, toep, x_cols, gm_send, gm_wide, gm_rows,
    gi_send, prod, gf_send, w_far, gm_far,
    far_ssem, far_psem, far_rsem, far_gsem, own_sem, load_sem, hop_send, hop_recv, x_send, x_recv, gm_ssem, gm_rsem, gi_ssem, gi_rsem, gf_ssem, gf_rsem,
):
    chips = chan_count // 2
    seq = lax.axis_index("seq")
    chan = lax.axis_index("chan")
    spot = chan // 2
    core = lax.rem(chan, 2)
    tok = go_hbm.shape[0]
    piece = tok // PARTS
    span_t = x_hbm.shape[0]
    rows = span_t * seq_count
    groups = f_ref.shape[0] // seq_count
    lags = f_ref.shape[1]
    used = min(lags, rows)
    own_ch = groups * width
    unit = 2 * tok
    count = rows // BLK
    span = rows + HALF
    depth = count * width
    cut = lags // seq_count

    up = {"chan": chan + 2}
    down = {"chan": chan - 2}
    twin = {"chan": chan + 1 - 2 * core}
    has_up = spot < chips - 1
    has_down = spot > 0

    upper = (2 * spot) // chips
    edge = spot + upper * (chips - 1 - 2 * spot)
    is_end = edge == 0 if chips >= 4 else spot < 0
    is_inner = edge == 1 if chips >= 4 else spot < 0
    mate = chan + (1 - 2 * upper) * (2 - 4 * edge)
    far = (1 - upper) * (chips - 1)
    far_parts = min(PARTS, own_ch // 16)
    far_rows = own_ch // far_parts

    def held(q):
        return jnp.logical_not(is_end & (q == far))

    def onward(q):
        return jnp.logical_not(is_inner & (q == far))

    def peer(r):
        return lax.rem(seq + r, seq_count)

    barrier = pltpu.get_barrier_semaphore()
    pl.semaphore_signal(barrier, inc=1, device_id=twin, device_id_type=MESH)
    for r in range(1, seq_count):
        pl.semaphore_signal(barrier, inc=1, device_id={"seq": peer(r)}, device_id_type=MESH)

    @pl.when(has_up)
    def _():
        pl.semaphore_signal(barrier, inc=1, device_id=up, device_id_type=MESH)

    @pl.when(has_down)
    def _():
        pl.semaphore_signal(barrier, inc=1, device_id=down, device_id_type=MESH)

    @pl.when(is_end | is_inner)
    def _():
        for r in range(1, seq_count):
            pl.semaphore_signal(
                barrier, inc=1, device_id={"seq": peer(r), "chan": mate}, device_id_type=MESH
            )

    load_own = pltpu.make_async_copy(
        go_hbm, gath.at[spot, pl.ds(core * tok, tok)], load_sem.at[0]
    )
    load_own.start()
    load_x = pltpu.make_async_copy(x_hbm, x_vm, load_sem.at[1])
    load_x.start()
    load_w = pltpu.make_async_copy(w_hbm, w_vm, load_sem.at[2])
    load_w.start()

    greeted = seq_count - 1 if chips >= 4 else 0

    @pl.when((edge == 1) & has_up & has_down)
    def _():
        pl.semaphore_wait(barrier, seq_count + 2 + greeted)

    @pl.when((edge > 1) & has_up & has_down)
    def _():
        pl.semaphore_wait(barrier, seq_count + 2)

    @pl.when(jnp.logical_not(has_up & has_down))
    def _():
        pl.semaphore_wait(barrier, seq_count + min(chips - 1, 1) + greeted)

    def slot(q, side, h):
        return gath.at[q, pl.ds(pl.multiple_of(side * tok + h * piece, piece), piece)]

    def hop(way, q, h, target):
        return pltpu.make_async_remote_copy(
            src_ref=slot(q, core, h),
            dst_ref=slot(q, core, h),
            send_sem=hop_send.at[way, q, h],
            recv_sem=hop_recv.at[q, core, h],
            device_id=target,
            device_id_type=MESH,
        )

    def arrived(q, side, h):
        pltpu.make_async_remote_copy(
            src_ref=slot(q, side, h),
            dst_ref=slot(q, side, h),
            send_sem=hop_send.at[2, q, h],
            recv_sem=hop_recv.at[q, side, h],
            device_id=twin,
            device_id_type=MESH,
        ).wait_recv()

    def far_span(s, h):
        return pl.ds(pl.multiple_of(s * own_ch + h * far_rows, far_rows), far_rows)

    def far_hop(h):
        return pltpu.make_async_remote_copy(
            src_ref=w_hbm.at[far_span(seq, h)],
            dst_ref=w_far.at[far_span(seq, h)],
            send_sem=far_ssem.at[h],
            recv_sem=far_rsem.at[seq, h],
            device_id={"chan": mate},
            device_id_type=MESH,
        )

    def far_share(source, target, h):
        return pltpu.make_async_remote_copy(
            src_ref=w_far.at[far_span(source, h)],
            dst_ref=w_far.at[far_span(source, h)],
            send_sem=far_psem.at[target, h],
            recv_sem=far_rsem.at[source, h],
            device_id={"seq": target},
            device_id_type=MESH,
        )

    def far_gm(source, target):
        return pltpu.make_async_remote_copy(
            src_ref=gm_far.at[pl.ds(pl.multiple_of(target * own_ch, own_ch), own_ch)],
            dst_ref=gm_wide.at[source * chips + far],
            send_sem=far_gsem.at[target],
            recv_sem=gm_rsem.at[far, source],
            device_id={"seq": target, "chan": mate},
            device_id_type=MESH,
        )

    @pl.when(is_end)
    def _():
        for h in range(far_parts):
            far_hop(h).start()

    load_own.wait()
    for h in range(PARTS):
        @pl.when(has_up)
        def _():
            hop(0, spot, h, up).start()

        @pl.when(has_down)
        def _():
            hop(1, spot, h, down).start()

    for h in range(PARTS):
        hop(2, spot, h, twin).start()

    load_x.wait()
    for i in range(0, x_vm.shape[1], HALF):
        x_turn[i : i + HALF, :] = x_vm[:, i : i + HALF].T

    def x_copy(source, target):
        return pltpu.make_async_remote_copy(
            src_ref=x_turn.at[pl.ds(pl.multiple_of(target * own_ch, own_ch), own_ch)],
            dst_ref=x_major.at[source],
            send_sem=x_send.at[target],
            recv_sem=x_recv.at[source],
            device_id={"seq": target},
            device_id_type=MESH,
        )

    for r in range(1, seq_count):
        x_copy(seq, peer(r)).start()
    x_major[seq] = x_turn[pl.ds(pl.multiple_of(seq * own_ch, own_ch), own_ch), :]

    for i in range(f_ref.shape[0]):
        taps[i] = f_ref[i : i + 1, :used].astype(jnp.float32)

    @pl.loop(0, groups)
    def _(g):
        pieces = [jnp.zeros((1, HALF), jnp.float32), taps[seq * groups + g]]
        if used < rows:
            pieces.append(jnp.zeros((1, rows - used), jnp.float32))
        line = jnp.concatenate(pieces, axis=1)
        base = jnp.concatenate(
            [line] + [pltpu.roll(line, r, 1) for r in range(1, SUB)], axis=0
        )
        for k in range(0, HALF // SUB, 2):
            low = base if k == 0 else pltpu.roll(base, k * SUB, 1)
            high = pltpu.roll(base, (k + 1) * SUB, 1)
            both = jnp.concatenate([low, high], axis=0).astype(jnp.bfloat16)
            toep[g, k * SUB : (k + 2) * SUB, HALF:] = both[:, HALF:]
        toep[g, :, :HALF] = jnp.zeros((HALF, HALF), jnp.bfloat16)

    def gm_copy(q, source, target):
        return pltpu.make_async_remote_copy(
            src_ref=gm_send.at[q, pl.ds(pl.multiple_of(target * own_ch, own_ch), own_ch)],
            dst_ref=gm_wide.at[source * chips + q],
            send_sem=gm_ssem.at[q, target],
            recv_sem=gm_rsem.at[q, source],
            device_id={"seq": target},
            device_id_type=MESH,
        )

    def project_far():
        for r in range(1, seq_count):
            for h in range(far_parts):
                far_share(peer(r), seq, h).wait_recv()
        gm_far[...] = lax.dot_general(
            w_far[...], gath[far], (((1,), (1,)), ((), ())), preferred_element_type=jnp.float32
        ).astype(jnp.bfloat16)
        for r in range(seq_count):
            far_gm(seq, peer(r)).start()

    def project(q):
        gm_send[q] = lax.dot_general(
            w_vm[...], gath[q], (((1,), (1,)), ((), ())), preferred_element_type=jnp.float32
        ).astype(jnp.bfloat16)
        for r in range(1, seq_count):
            gm_copy(q, seq, peer(r)).start()
        gm_wide[seq * chips + q] = gm_send[
            q, pl.ds(pl.multiple_of(seq * own_ch, own_ch), own_ch), :
        ]

    load_w.wait()
    for r in range(1, seq_count):
        x_copy(peer(r), seq).wait_recv()

    @pl.loop(0, groups)
    def _(g):
        first = pl.multiple_of(g * width, width)
        per = span_t // BLK
        x_rows = jnp.concatenate(
            [
                x_major[a // per, pl.ds(first, width), (a % per) * BLK : (a % per + 1) * BLK]
                for a in range(count)
            ],
            axis=0,
        )
        x_cols[g] = x_rows.T

    def relay(d):
        for h in range(far_parts):
            @pl.when(is_inner & (d == 1))
            def _():
                far_hop(h).wait_recv()
                for r in range(1, seq_count):
                    far_share(seq, peer(r), h).start()

        for h in range(PARTS):
            @pl.when((spot >= d) & held(spot - d))
            def _():
                arrived(spot - d, core, h)

                @pl.when(has_up & onward(spot - d))
                def _():
                    hop(0, spot - d, h, up).start()

                hop(2, spot - d, h, twin).start()

            @pl.when((spot + d < chips) & held(spot + d))
            def _():
                arrived(spot + d, core, h)

                @pl.when(has_down & onward(spot + d))
                def _():
                    hop(1, spot + d, h, down).start()

                hop(2, spot + d, h, twin).start()

    @pl.loop(0, chips)
    def _(d):
        @pl.when(d > 0)
        def _():
            relay(d)

        @pl.loop(0, 2)
        def _(side):
            q = spot - d + 2 * d * side

            @pl.when((q >= 0) & (q < chips) & (d + 1 - side > 0) & held(q))
            def _():
                for h in range(PARTS):
                    arrived(q, 1 - core, h)

                @pl.when(is_inner & (q == far))
                def _():
                    project_far()

                project(q)

    @pl.loop(0, chips)
    def _(q):
        for r in range(1, seq_count):
            gm_copy(q, peer(r), seq).wait_recv()

        @pl.when(is_end & (q == far))
        def _():
            far_gm(seq, seq).wait_recv()

    def gi_copy(g, source, target):
        return pltpu.make_async_remote_copy(
            src_ref=gi_send.at[target, g],
            dst_ref=gi_out.at[source, g],
            send_sem=gi_ssem.at[g, target],
            recv_sem=gi_rsem.at[g, source],
            device_id={"seq": target},
            device_id_type=MESH,
        )

    def gf_copy(source, target):
        return pltpu.make_async_remote_copy(
            src_ref=gf_send.at[target],
            dst_ref=gf_out.at[source],
            send_sem=gf_ssem.at[target],
            recv_sem=gf_rsem.at[source],
            device_id={"seq": target},
            device_id_type=MESH,
        )

    @pl.loop(0, groups)
    def _(g):
        first = pl.multiple_of(g * width, width)
        fold = BLK // unit
        for a in range(count):
            for u in range(fold):
                gm_rows[g, a * width : (a + 1) * width, u * unit : (u + 1) * unit] = gm_wide[
                    a * fold + u, pl.ds(first, width), :
                ]
        gm_rows[g, depth:, :] = jnp.zeros((depth, BLK), jnp.bfloat16)

        step = min(4, count)
        total = None
        for j in range(0, count, step):
            m = (count - j) * width
            left = jnp.concatenate(
                [gm_rows[g, (j + q) * width : (j + q) * width + m, :] for q in range(step)], axis=1
            )
            right = jnp.concatenate(
                [
                    toep[g, :, HALF + j * BLK : HALF + (j + step) * BLK],
                    toep[g, :, j * BLK : (j + step) * BLK],
                ],
                axis=0,
            )
            part = lax.dot_general(
                left, right, (((1,), (1,)), ((), ())), preferred_element_type=jnp.float32
            )
            if total is None:
                total = part
            else:
                total = jnp.concatenate([total[:m] + part, total[m:]], axis=0)
        per = span_t // BLK
        for a in range(count):
            gi_send[a // per, g, :, (a % per) * BLK : (a % per + 1) * BLK] = total[
                a * width : (a + 1) * width
            ].astype(jnp.bfloat16)
        for r in range(1, seq_count):
            gi_copy(g, seq, peer(r)).start()
        pltpu.make_async_copy(gi_send.at[seq, g], gi_out.at[seq, g], own_sem.at[g]).start()

    @pl.loop(0, groups)
    def _(g):

        prod[:, :HALF] = jnp.zeros((HALF, HALF), jnp.float32)
        for j in range(count):
            k = min(depth, -(-((count - j) * width) // BLK) * BLK)
            part = jnp.dot(
                x_cols[g, :, :k],
                gm_rows[g, j * width : j * width + k, :],
                preferred_element_type=jnp.float32,
            )
            lo = j * BLK
            if j:
                prod[:, lo : lo + HALF] += part[HALF:, :HALF]
            prod[:, lo + HALF : lo + BLK] = part[:HALF, :HALF] + part[HALF:, HALF:]
            prod[:, lo + BLK : lo + BLK + HALF] = part[:HALF, HALF:]
        acc = prod[:SUB, :]
        for k in range(1, HALF // SUB):
            acc = acc + pltpu.roll(prod[k * SUB : (k + 1) * SUB, :], span - k * SUB, 1)
        out = acc[:1]
        for r in range(1, SUB):
            out = out + pltpu.roll(acc[r : r + 1], span - r, 1)
        for s in range(seq_count):
            live = min(max(used - s * cut, 0), cut)
            if live:
                gf_send[s, g, :, :live] = out[:, HALF + s * cut : HALF + s * cut + live]
            if live < cut:
                gf_send[s, g, :, live:] = jnp.zeros((1, cut - live), jnp.float32)

    for r in range(1, seq_count):
        gf_copy(seq, peer(r)).start()
    own_gf = pltpu.make_async_copy(gf_send.at[seq], gf_out.at[seq], own_sem.at[groups])
    own_gf.start()

    @pl.loop(0, groups)
    def _(g):
        for r in range(1, seq_count):
            gi_copy(g, peer(r), seq).wait_recv()

    for r in range(1, seq_count):
        gf_copy(peer(r), seq).wait_recv()
    own_gf.wait()

    for r in range(1, seq_count):
        x_copy(seq, peer(r)).wait_send()
        gf_copy(seq, peer(r)).wait_send()

    @pl.loop(0, groups)
    def _(g):
        for r in range(1, seq_count):
            gi_copy(g, seq, peer(r)).wait_send()
        pltpu.make_async_copy(gi_send.at[seq, g], gi_out.at[seq, g], own_sem.at[g]).wait()

    @pl.loop(0, chips)
    def _(q):
        @pl.when(held(q))
        def _():
            for r in range(1, seq_count):
                gm_copy(q, seq, peer(r)).wait_send()
            for h in range(PARTS):
                hop(2, q, h, twin).wait_send()

        for h in range(PARTS):
            @pl.when(has_up & (q <= spot) & held(q) & onward(q))
            def _():
                hop(0, q, h, up).wait_send()

            @pl.when(has_down & (q >= spot) & held(q) & onward(q))
            def _():
                hop(1, q, h, down).wait_send()

    @pl.when(is_end)
    def _():
        for h in range(far_parts):
            far_hop(h).wait_send()

    @pl.when(is_inner)
    def _():
        for r in range(1, seq_count):
            for h in range(far_parts):
                far_share(seq, peer(r), h).wait_send()
        for r in range(seq_count):
            far_gm(seq, peer(r)).wait_send()


def on_device(chan_count, seq_count, conv_input, grad_out, out_weight, filters):
    span_t, chans = conv_input.shape
    tok, model = grad_out.shape
    all_groups, lags = filters.shape
    width = chans // all_groups
    groups = all_groups // seq_count
    own_ch = groups * width
    rows = span_t * seq_count
    chips = chan_count // 2
    unit = 2 * tok
    count = rows // BLK
    depth = count * width
    cut = lags // seq_count
    used = min(lags, rows)
    bf16, f32 = jnp.bfloat16, jnp.float32
    dma = pltpu.SemaphoreType.DMA
    hbm = pl.BlockSpec(memory_space=pl.ANY)
    vmem = pl.BlockSpec(memory_space=pltpu.VMEM)
    work = chans * rows * model // seq_count + 2 * own_ch * rows * rows
    through, lagged = pl.pallas_call(
        functools.partial(whole_kernel, chan_count, seq_count, width),
        out_shape=(
            jax.ShapeDtypeStruct((seq_count, groups, width, span_t), bf16),
            jax.ShapeDtypeStruct((seq_count, groups, 1, cut), f32),
        ),
        in_specs=[hbm, hbm, hbm, vmem],
        out_specs=(hbm, hbm),
        scratch_shapes=[
            pltpu.VMEM((chips, unit, model), bf16),
            pltpu.VMEM(out_weight.shape, bf16),
            pltpu.VMEM((span_t, chans), bf16),
            pltpu.VMEM((chans, span_t), bf16),
            pltpu.VMEM((seq_count, own_ch, span_t), bf16),
            pltpu.VMEM((all_groups, 1, used), f32),
            pltpu.VMEM((groups, HALF, rows + HALF), bf16),
            pltpu.VMEM((groups, BLK, depth), bf16),
            pltpu.VMEM((chips, chans, unit), bf16),
            pltpu.VMEM((seq_count * chips, own_ch, unit), bf16),
            pltpu.VMEM((groups, 2 * depth, BLK), bf16),
            pltpu.VMEM((seq_count, groups, width, span_t), bf16),
            pltpu.VMEM((HALF, rows + HALF), f32),
            pltpu.VMEM((seq_count, groups, 1, cut), f32),
            pltpu.VMEM(out_weight.shape, bf16),
            pltpu.VMEM((chans, unit), bf16),
            dma((PARTS,)),
            dma((seq_count, PARTS)),
            dma((seq_count, PARTS)),
            dma((seq_count,)),
            dma((groups + 1,)),
            dma((3,)),
            dma((3, chips, PARTS)),
            dma((chips, 2, PARTS)),
            dma((seq_count,)),
            dma((seq_count,)),
            dma((chips, seq_count)),
            dma((chips, seq_count)),
            dma((groups, seq_count)),
            dma((groups, seq_count)),
            dma((seq_count,)),
            dma((seq_count,)),
        ],
        cost_estimate=pl.CostEstimate(
            flops=2 * work, bytes_accessed=16 * 1024 * 1024, transcendentals=0
        ),
        compiler_params=pltpu.CompilerParams(
            vmem_limit_bytes=56 * 1024 * 1024, collective_id=0, has_side_effects=True
        ),
    )(conv_input, grad_out, out_weight, filters)
    return through.reshape(chans, span_t).T, lagged.reshape(all_groups, cut)


def solution(mesh):
    in_specs = (P("seq", "chan"), P(("seq", "chan"), None), P("chan", None), P("chan", None))
    out_specs = (P("seq", "chan"), P("chan", "seq"))
    return jax.shard_map(
        functools.partial(on_device, mesh.shape["chan"], mesh.shape["seq"]),
        mesh=mesh, in_specs=in_specs, out_specs=out_specs, check_vma=False,
    )
```
